512 devices in a mesh: pipe: 8 (over x, core), dp: 64 (over y, z).
Axes of the slice: x: 4, y: 4, z: 16, core: 2. Of those that a mesh axis runs over, the one named last changes fastest.
Arguments:
- hidden_in: bfloat16 [8, 8192, 4096], P('pipe', 'dp'), may hold values from -20 to 20
- norm_gain: float32 [8, 2, 4096], P('pipe'), may hold values from 0.5 to 1.5
- self_kv: bfloat16 [8, 2, 8192, 1024], P('pipe', None, 'dp'), may hold values from -6 to 6
- prefix_kv: bfloat16 [8, 2, 8192, 1024], P('pipe', None, 'dp'), may hold values from -7 to 7
- partner_prefix: int32 [64], P('dp'), may hold values from 0 to 62, as said below
- resp_len: int32 [64], P('dp'), may hold values from 1 to 128, as said below
Outputs:
- hidden_out: bfloat16 [8, 8192, 4096], P('pipe', 'dp')
The draws below stay inside these ranges and needn't reach their ends.
Inputs may be any that keep to these rules, and one draw needn't show every extreme that they name: 0 <= i - partner_prefix[i] <= 3 for every slot i, and a difference of 3 occurs in every draw. `resp_len`: the value 128 occurs in every draw.
All inputs are finite; a program needn't handle non-finite values.
Results may differ from the reference program's by a relative error of at most 0.012.
Values may be sent and summed in bfloat16 or wider, within the bound.
A program may use at most 64 MiB of HBM per device.

```python
import jax
import jax.numpy as jnp
from jax import lax

HEADS = 32
KV_HEADS = 4
HEAD_DIM = 128
LAYERS = 2
REACH = 4
RESP = 128
PRE = 128
WIN = 4096
KVW = 1024
SECTIONS = 8
OWNERS = 64
TOKENS = 8192
PRE_ROWS = 8192


def draw_hidden_in(key, part):
    key = jax.random.fold_in(key, 1)
    first = jax.random.fold_in(key, 0)
    base = jnp.clip(jax.random.normal(first, (SECTIONS, TOKENS, WIN), jnp.float32), -6.0, 6.0)
    return base.astype(jnp.bfloat16)


def draw_prefix_kv(key, part):
    key = jax.random.fold_in(key, 2)
    first = jax.random.fold_in(key, 0)
    base = jnp.clip(jax.random.normal(first, (SECTIONS, LAYERS, PRE_ROWS, KVW), jnp.float32), -6.0, 6.0)
    return base.astype(jnp.bfloat16)


def draw_partner_prefix(key, part):
    key = jax.random.fold_in(key, 3)
    places = jnp.arange(OWNERS, dtype=jnp.int32)
    offsets = jax.random.randint(key, (OWNERS,), 0, REACH, jnp.int32)
    offsets = jnp.where(places == OWNERS - 2, 0, offsets)
    offsets = jnp.where(places == OWNERS - 1, REACH - 1, offsets)
    offsets = jnp.minimum(offsets, places)
    return (places - offsets).astype(jnp.int32)


def draw_resp_len(key, part):
    key = jax.random.fold_in(key, 4)
    first, second = jax.random.split(key)
    lengths = jax.random.randint(first, (OWNERS,), 1, RESP + 1, jnp.int32)
    picked = jax.random.randint(second, (), 0, OWNERS, jnp.int32)
    return jnp.where(jnp.arange(OWNERS, dtype=jnp.int32) == picked, RESP, lengths).astype(jnp.int32)


def block_levels(rng, shape, cuts, smallest, top_value):
    level = 1.0
    for position, parts in cuts:
        heights = jax.random.uniform(jax.random.fold_in(jax.random.fold_in(rng, 6), position), (parts,), jnp.float32, smallest / len(cuts), top_value / len(cuts))
        level = level * jnp.repeat(jnp.exp(heights), shape[position] // parts).reshape((-1,) + (1,) * (len(shape) - 1 - position))
    return level


def bell_draw(key, dims, deviation, bound, cuts=(), held_as=jnp.bfloat16):
    entries = deviation * jax.random.normal(key, dims, jnp.float32)
    if cuts:
        entries = entries * block_levels(key, dims, cuts, -0.22, 0.18)
    return jnp.clip(entries, -bound, bound).astype(held_as)


def setup_inputs(seed: int = 0) -> dict:
    streams_of = jax.random.split(jax.random.key(seed), 7)
    return {
        "hidden_in": draw_hidden_in(jax.random.fold_in(streams_of[6], 71), 0),
        "norm_gain": jnp.clip(1.0 + 0.1 * jax.random.normal(streams_of[1], (SECTIONS, LAYERS, WIN), jnp.float32), 0.5, 1.5),
        "self_kv": bell_draw(streams_of[2], (SECTIONS, LAYERS, TOKENS, KVW), 1.0, 6.0, ((0, 8), (2, 64))),
        "prefix_kv": draw_prefix_kv(jax.random.fold_in(streams_of[6], 71), 0),
        "partner_prefix": draw_partner_prefix(jax.random.fold_in(streams_of[6], 71), 0),
        "resp_len": draw_resp_len(jax.random.fold_in(streams_of[6], 71), 0),
    }


def one_layer(hidden, gain, own_kv, pre_kv, length):
    x = hidden.astype(jnp.float32)
    normed = x * lax.rsqrt(lax.optimization_barrier(jnp.mean(x * x, axis=-1, keepdims=True)) + 1e-05) * gain
    rows = x.shape[0]
    query = normed.astype(jnp.bfloat16).astype(jnp.float32).reshape(rows, KV_HEADS, HEADS // KV_HEADS, HEAD_DIM)
    keys_all = jnp.concatenate([pre_kv, own_kv], axis=0).astype(jnp.float32)
    span = keys_all.shape[0]
    keys = keys_all[:, :KV_HEADS * HEAD_DIM].reshape(span, KV_HEADS, HEAD_DIM)
    values = keys_all[:, KV_HEADS * HEAD_DIM:].reshape(span, KV_HEADS, HEAD_DIM)
    scores = jnp.einsum('rkgd,skd->kgrs', query, keys) / jnp.sqrt(jnp.float32(HEAD_DIM))
    row_pos = jnp.arange(rows)[:, None]
    key_pos = jnp.arange(span)[None, :] - PRE
    seen = (key_pos < 0) | (key_pos <= row_pos) & (key_pos < length)
    scores = jnp.where(seen, scores, jnp.float32(-1e+30))
    top = lax.optimization_barrier(jnp.max(scores, axis=-1, keepdims=True))
    expo = jnp.exp(scores - top)
    weights = (expo / lax.optimization_barrier(jnp.sum(expo, axis=-1, keepdims=True))).astype(jnp.bfloat16).astype(jnp.float32)
    mixed = jnp.einsum('kgrs,skd->rkgd', weights, values).reshape(rows, HEADS * HEAD_DIM)
    return (x + mixed).astype(jnp.bfloat16)

def reference(hidden_in, norm_gain, self_kv, prefix_kv, partner_prefix, resp_len):
    results = []
    for section in range(SECTIONS):
        hidden = hidden_in[section].reshape(OWNERS, RESP, WIN)
        for layer in range(LAYERS):
            pre_all = prefix_kv[section, layer].reshape(OWNERS, PRE, KVW)[partner_prefix.astype(jnp.int32)]
            own_all = self_kv[section, layer].reshape(OWNERS, RESP, KVW)
            gain = norm_gain[section, layer]
            hidden = lax.map(lambda item: one_layer(item[0], gain, item[1], item[2], item[3]), (hidden, own_all, pre_all, resp_len))
        results.append(hidden.reshape(TOKENS, WIN))
    stacked = jnp.stack(results)
    return jnp.roll(stacked, 1, axis=0)
```

```python
import math

import jax
import jax.numpy as jnp
from jax import lax
from jax.experimental import pallas as pl
from jax.experimental.pallas import tpu as pltpu
from jax.sharding import PartitionSpec as P

HEADS = 32
KV_HEADS = 4
GROUP = HEADS // KV_HEADS
HEAD_DIM = 128
LAYERS = 2
REACH = 4
RESP = 128
WIN = HEADS * HEAD_DIM
KVW = 2 * KV_HEADS * HEAD_DIM
HALF = KVW // 2
PIECES = 2 * KV_HEADS
SCALE = math.log2(math.e) / math.sqrt(HEAD_DIM)
OUT_PARTS = 8
PART = WIN // OUT_PARTS
MESH = pl.DeviceIdType.MESH


def kernel(hid_ref, gain_ref, own_ref, pre_ref, partner, length, out_ref,
           h, q, own, gain, pre, kcat, vcat, bias, squares,
           load_sem, slot_sem, send_sem, recv_sem, out_send, out_recv):
    pipe, dp = lax.axis_index("pipe"), lax.axis_index("dp")
    sections, owners = lax.axis_size("pipe"), lax.axis_size("dp")
    right = (pipe, lax.rem(dp + 1, owners))
    left = (pipe, lax.rem(dp + owners - 1, owners))
    onward = (lax.rem(pipe + 1, sections), dp)
    back = (lax.rem(pipe + sections - 1, sections), dp)

    barrier = pltpu.get_barrier_semaphore()
    for device in (left, back):
        pl.semaphore_signal(barrier, inc=1, device_id=device, device_id_type=MESH)

    def column(piece):
        return (piece % 2) * HALF + (piece // 2) * HEAD_DIM

    def owned(layer, piece):
        return pre_ref.at[0, layer, :, pl.ds(column(piece), HEAD_DIM)]

    loads = [
        pltpu.make_async_copy(hid_ref.at[0], h, load_sem.at[0]),
        pltpu.make_async_copy(gain_ref.at[0], gain, load_sem.at[1]),
        pltpu.make_async_copy(own_ref.at[0], own, load_sem.at[2]),
    ]
    slots = [
        pltpu.make_async_copy(owned(layer, piece), pre.at[layer, piece, 0], slot_sem.at[layer, piece])
        for layer in range(LAYERS)
        for piece in range(PIECES)
    ]
    for copy in loads:
        copy.start()
    pl.semaphore_wait(barrier, 2)

    def hop(layer, piece, step):
        source = owned(layer, piece) if step == 1 else pre.at[layer, piece, step - 1]
        return pltpu.make_async_remote_copy(
            src_ref=source,
            dst_ref=pre.at[layer, piece, step],
            send_sem=send_sem.at[layer, piece, step - 1],
            recv_sem=recv_sem.at[layer, piece, step - 1],
            device_id=right,
            device_id_type=MESH,
        )

    def forward(layer, pieces, step):
        for piece in pieces:
            if step > 1:
                hop(layer, piece, step - 1).wait_recv()
            hop(layer, piece, step).start()

    def handed(part):
        columns = pl.ds(part * PART, PART)
        return pltpu.make_async_remote_copy(
            src_ref=h.at[:, columns],
            dst_ref=out_ref.at[0, :, columns],
            send_sem=out_send.at[part],
            recv_sem=out_recv.at[part],
            device_id=onward,
            device_id_type=MESH,
        )

    def head_columns(head):
        return pl.ds(pl.multiple_of(head * HEAD_DIM, HEAD_DIM), HEAD_DIM)

    def add_squares():
        squares[...] = jnp.zeros_like(squares)

        @pl.loop(0, HEADS // GROUP)
        def _(group):
            summed = squares[...]
            for within in range(GROUP):
                x = h[:, head_columns(group * GROUP + within)].astype(jnp.float32)
                summed = summed + x * x
            squares[...] = summed

    def queries(layer):
        mean = jnp.sum(squares[...], axis=-1, keepdims=True) * (1.0 / WIN)
        factor = jnp.broadcast_to(lax.rsqrt(mean + 1e-05), (RESP, HEAD_DIM))

        @pl.loop(0, HEADS // GROUP)
        def _(group):
            for within in range(GROUP):
                columns = head_columns(group * GROUP + within)
                x = h[:, columns].astype(jnp.float32)
                q[:, columns] = (x * factor * gain[pl.ds(layer, 1), columns]).astype(jnp.bfloat16)

    def chosen(layer, piece):
        offset = dp - partner[0]
        block = pre[layer, piece, 0]
        for step in range(1, REACH):
            block = jnp.where(offset == step, pre[layer, piece, step], block)
        return block

    def mix(columns):
        scores = lax.dot_general(
            q[:, columns], kcat[...], (((1,), (1,)), ((), ())), preferred_element_type=jnp.float32
        )
        scores = scores * SCALE + bias[...]
        top = jnp.max(scores, axis=-1, keepdims=True)
        expo = jnp.exp2(scores - top).astype(jnp.bfloat16)
        mixed = jnp.dot(expo, vcat[...], preferred_element_type=jnp.float32)
        return mixed[:, :HEAD_DIM] / mixed[:, HEAD_DIM:]

    def attend(layer, group, first, last):
        heads = [pl.ds((group * GROUP + within) * HEAD_DIM, HEAD_DIM) for within in range(first, last)]
        mixes = [mix(columns) for columns in heads]
        summed = squares[...] if layer + 1 < LAYERS else None
        for columns, mixed in zip(heads, mixes):
            total = (h[:, columns].astype(jnp.float32) + mixed).astype(jnp.bfloat16)
            h[:, columns] = total
            if layer + 1 < LAYERS:
                x = total.astype(jnp.float32)
                summed = summed + x * x
        if layer + 1 < LAYERS:
            squares[...] = summed

    def settle(layer, group):
        for piece in (2 * group, 2 * group + 1):
            hop(layer, piece, REACH - 1).wait_recv()
            slots[layer * PIECES + piece].wait()
        kcat[pl.ds(0, RESP), :] = chosen(layer, 2 * group)
        kcat[pl.ds(RESP, RESP), :] = own[layer, :, pl.ds(group * HEAD_DIM, HEAD_DIM)]
        vcat[pl.ds(0, RESP), pl.ds(0, HEAD_DIM)] = chosen(layer, 2 * group + 1)
        vcat[pl.ds(RESP, RESP), pl.ds(0, HEAD_DIM)] = own[layer, :, pl.ds(HALF + group * HEAD_DIM, HEAD_DIM)]

    every = range(PIECES)
    forward(0, every, 1)
    for copy in slots:
        copy.start()
    vcat[:, pl.ds(HEAD_DIM, HEAD_DIM)] = jnp.ones((2 * RESP, HEAD_DIM), jnp.bfloat16)
    for copy in loads:
        copy.wait()
    row = lax.broadcasted_iota(jnp.int32, (RESP, RESP), 0)
    key = lax.broadcasted_iota(jnp.int32, (RESP, RESP), 1)
    seen = (key <= row) & (key < length[0])
    bias[:, pl.ds(0, RESP)] = jnp.zeros((RESP, RESP), jnp.float32)
    bias[:, pl.ds(RESP, RESP)] = jnp.where(seen, 0.0, -1e30)
    forward(0, every[:4], 2)
    add_squares()
    queries(0)
    squares[...] = jnp.zeros_like(squares)
    forward(0, every[4:], 2)
    forward(0, every, 3)
    forward(1, every, 1)
    for group in range(KV_HEADS):
        settle(0, group)
        attend(0, group, 0, GROUP)
        forward(1, every[2 * group : 2 * group + 2], 2)
    queries(1)
    forward(1, every, 3)
    for group in range(KV_HEADS):
        settle(1, group)
        for half in range(2):
            attend(1, group, half * GROUP // 2, (half + 1) * GROUP // 2)
            handed(2 * group + half).start()

    for layer in range(LAYERS):
        for piece in range(PIECES):
            for step in range(1, REACH):
                hop(layer, piece, step).wait_send()
    for part in range(OUT_PARTS):
        handed(part).wait()


def per_device(hidden_in, norm_gain, self_kv, prefix_kv, partner_prefix, resp_len):
    hbm = pl.BlockSpec(memory_space=pltpu.HBM)
    bf16, f32 = jnp.bfloat16, jnp.float32
    smem = pl.BlockSpec(memory_space=pltpu.SMEM)
    large = [
        pltpu.with_memory_space_constraint(array, pltpu.HBM)
        for array in (hidden_in, norm_gain, self_kv, prefix_kv)
    ]
    return pl.pallas_call(
        kernel,
        out_shape=pltpu.VMEM((1, RESP, WIN), bf16),
        in_specs=[hbm] * 4 + [smem] * 2,
        out_specs=pl.BlockSpec(memory_space=pltpu.VMEM),
        scratch_shapes=[
            pltpu.VMEM((RESP, WIN), bf16),
            pltpu.VMEM((RESP, WIN), bf16),
            pltpu.VMEM((LAYERS, RESP, KVW), bf16),
            pltpu.VMEM((LAYERS, WIN), f32),
            pltpu.VMEM((LAYERS, PIECES, REACH, RESP, HEAD_DIM), bf16),
            pltpu.VMEM((2 * RESP, HEAD_DIM), bf16),
            pltpu.VMEM((2 * RESP, 2 * HEAD_DIM), bf16),
            pltpu.VMEM((RESP, 2 * RESP), f32),
            pltpu.VMEM((RESP, HEAD_DIM), f32),
            pltpu.SemaphoreType.DMA((3,)),
            pltpu.SemaphoreType.DMA((LAYERS, PIECES)),
            pltpu.SemaphoreType.DMA((LAYERS, PIECES, REACH - 1)),
            pltpu.SemaphoreType.DMA((LAYERS, PIECES, REACH - 1)),
            pltpu.SemaphoreType.DMA((OUT_PARTS,)),
            pltpu.SemaphoreType.DMA((OUT_PARTS,)),
        ],
        compiler_params=pltpu.CompilerParams(
            collective_id=0, has_side_effects=True, vmem_limit_bytes=48 * 2**20
        ),
        name="judge",
    )(*large, partner_prefix, resp_len)


def solution(mesh):
    return jax.shard_map(
        per_device,
        mesh=mesh,
        in_specs=(
            P("pipe", "dp", None),
            P("pipe", None, None),
            P("pipe", None, "dp", None),
            P("pipe", None, "dp", None),
            P("dp"),
            P("dp"),
        ),
        out_specs=P("pipe", "dp", None),
        check_vma=False,
    )
```

```python
import math

import jax
import jax.numpy as jnp
from jax import lax
from jax.experimental import pallas as pl
from jax.experimental.pallas import tpu as pltpu
from jax.sharding import PartitionSpec as P

HEADS = 32
KV_HEADS = 4
GROUP = HEADS // KV_HEADS
HEAD_DIM = 128
LAYERS = 2
REACH = 4
RESP = 128
WIN = HEADS * HEAD_DIM
KVW = 2 * KV_HEADS * HEAD_DIM
HALF = KVW // 2
PIECES = 2 * KV_HEADS
SCALE = math.log2(math.e) / math.sqrt(HEAD_DIM)
OUT_PARTS = KV_HEADS
PART = WIN // OUT_PARTS
MESH = pl.DeviceIdType.MESH
DEPTH = 16
WAYS = 4
LAG = 2
HEAD_START = 5
SLOTS = [(layer, group, step) for step in range(1, REACH) for layer in range(LAYERS) for group in range(KV_HEADS)]


def kernel(hid_ref, gain_ref, own_ref, pre_ref, partner, length, out_ref,
           h, own, gain, pre, kcat, vcat, bias, squares, factor,
           way, turn, load_sem, slot_sem, send_sem, recv_sem, way_send, way_recv, out_send, out_recv):
    pipe, dp = lax.axis_index("pipe"), lax.axis_index("dp")
    sections, owners = lax.axis_size("pipe"), lax.axis_size("dp")
    right = (pipe, lax.rem(dp + 1, owners))
    left = (pipe, lax.rem(dp + owners - 1, owners))
    below = (pipe, lax.rem(dp + DEPTH, owners))
    above = (pipe, lax.rem(dp + owners - DEPTH, owners))
    start_of_row = (pipe, lax.rem(dp + owners - DEPTH + 1, owners))
    onward = (lax.rem(pipe + 1, sections), dp)
    back = (lax.rem(pipe + sections - 1, sections), dp)

    y, z = dp // DEPTH, dp % DEPTH
    low, high = z == 0, z == DEPTH - 1
    flows = high & (dp < owners - 1)
    relays = high & (y > 0)

    barrier = pltpu.get_barrier_semaphore()
    pl.semaphore_signal(barrier, inc=1, device_id=back, device_id_type=MESH)

    @pl.when(pipe % 2 == 0)
    def _():
        pl.semaphore_signal(barrier, inc=1, device_id=onward, device_id_type=MESH)

    @pl.when(dp > 0)
    def _():
        pl.semaphore_signal(barrier, inc=1, device_id=left, device_id_type=MESH)

    @pl.when(relays)
    def _():
        pl.semaphore_signal(barrier, inc=1, device_id=above, device_id_type=MESH)

    @pl.when(low & (y > 0))
    def _():
        pl.semaphore_signal(barrier, inc=1, device_id=(pipe, dp + DEPTH - 1), device_id_type=MESH)

    def column(piece):
        return (piece % 2) * HALF + (piece // 2) * HEAD_DIM

    def owned(layer, piece):
        return pre_ref.at[0, layer, :, pl.ds(column(piece), HEAD_DIM)]

    loads = [
        pltpu.make_async_copy(hid_ref.at[0], h, load_sem.at[0]),
        pltpu.make_async_copy(gain_ref.at[0], gain, load_sem.at[1]),
        pltpu.make_async_copy(own_ref.at[0], own, load_sem.at[2]),
    ]
    slots = [
        pltpu.make_async_copy(owned(layer, piece), pre.at[layer, piece, 0], slot_sem.at[layer, piece])
        for layer in range(LAYERS)
        for piece in range(PIECES)
    ]
    for copy in loads:
        copy.start()
    odd = pipe % 2 == 1
    greeted = 1 + sum(condition.astype(jnp.int32) for condition in (odd, dp < owners - 1, flows, relays))
    pl.semaphore_wait(barrier, greeted)

    def hop(layer, piece, step):
        source = owned(layer, piece) if step == 1 else pre.at[layer, piece, step - 1]
        return pltpu.make_async_remote_copy(
            src_ref=source,
            dst_ref=pre.at[layer, piece, step],
            send_sem=send_sem.at[layer, piece, step - 1],
            recv_sem=recv_sem.at[layer, piece, step - 1],
            device_id=right,
            device_id_type=MESH,
        )

    def aside(layer, piece, step):
        source = owned(layer, piece) if step == 1 else pre.at[layer, piece, step - 1]
        return pltpu.make_async_remote_copy(
            src_ref=source,
            dst_ref=way.at[layer, piece, step - 1],
            send_sem=send_sem.at[layer, piece, step - 1],
            recv_sem=way_recv.at[layer, piece, step - 1],
            device_id=below,
            device_id_type=MESH,
        )

    def relayed(layer, piece, step):
        return pltpu.make_async_remote_copy(
            src_ref=way.at[layer, piece, step - 1],
            dst_ref=pre.at[layer, piece, step],
            send_sem=way_send.at[layer, piece, step - 1],
            recv_sem=recv_sem.at[layer, piece, step - 1],
            device_id=start_of_row,
            device_id_type=MESH,
        )

    def pieces_of(group):
        return 2 * group, 2 * group + 1

    def arrive(layer, group, step):
        @pl.when(dp >= step)
        def _():
            for piece in pieces_of(group):
                hop(layer, piece, step).wait_recv()

    def forward(layer, group, step):
        if step > 1:
            arrive(layer, group, step - 1)

        @pl.when((dp >= step - 1) & (z < DEPTH - 1))
        def _():
            for piece in pieces_of(group):
                hop(layer, piece, step).start()

        @pl.when(flows)
        def _():
            for piece in pieces_of(group):
                rank = piece % WAYS

                @pl.when(y < rank)
                def _():
                    hop(layer, piece, step).start()

                if rank < WAYS - 1:

                    @pl.when(y >= rank)
                    def _():
                        aside(layer, piece, step).start()

    def relay(layer, group, step, sent=False):
        @pl.when(relays)
        def _():
            for piece in pieces_of(group):
                rank = piece % WAYS
                if rank < WAYS - 1:

                    @pl.when(y > rank)
                    def _():
                        if sent:
                            relayed(layer, piece, step).wait_send()
                        else:
                            aside(layer, piece, step).wait_recv()
                            relayed(layer, piece, step).start()

    def sent(layer, group, step):
        early = step == 1 and (layer, group, step) in SLOTS[:HEAD_START]
        @pl.when((dp >= step - 1) & (dp < owners - 1) & (jnp.logical_not(odd) if early else True))
        def _():
            for piece in pieces_of(group):
                hop(layer, piece, step).wait_send()

    def handed(part):
        columns = pl.ds(part * PART, PART)
        return pltpu.make_async_remote_copy(
            src_ref=h.at[:, columns],
            dst_ref=out_ref.at[0, :, columns],
            send_sem=out_send.at[part],
            recv_sem=out_recv.at[part],
            device_id=onward,
            device_id_type=MESH,
        )

    def head_columns(head):
        return pl.ds(pl.multiple_of(head * HEAD_DIM, HEAD_DIM), HEAD_DIM)

    def add_squares():
        squares[...] = jnp.zeros_like(squares)

        @pl.loop(0, HEADS // GROUP)
        def _(group):
            summed = squares[...]
            for within in range(GROUP):
                x = h[:, head_columns(group * GROUP + within)].astype(jnp.float32)
                summed = summed + x * x
            squares[...] = summed

    def settle_norm():
        mean = jnp.sum(squares[...], axis=-1, keepdims=True) * (1.0 / WIN)
        factor[...] = jnp.broadcast_to(lax.rsqrt(mean + 1e-05), (RESP, HEAD_DIM))

    def chosen(layer, piece):
        offset = dp - partner[0]
        block = pre[layer, piece, 0]
        for step in range(1, REACH):
            block = jnp.where(offset == step, pre[layer, piece, step], block)
        return block

    def mix(layer, columns):
        x = h[:, columns].astype(jnp.float32)
        query = (x * factor[...] * gain[pl.ds(layer, 1), columns]).astype(jnp.bfloat16)
        scores = lax.dot_general(
            query, kcat[...], (((1,), (1,)), ((), ())), preferred_element_type=jnp.float32
        )
        scores = scores * SCALE + bias[...]
        top = jnp.max(scores, axis=-1, keepdims=True)
        expo = jnp.exp2(scores - top).astype(jnp.bfloat16)
        mixed = jnp.dot(expo, vcat[...], preferred_element_type=jnp.float32)
        return (x + mixed[:, :HEAD_DIM] / mixed[:, HEAD_DIM:]).astype(jnp.bfloat16)

    def attend(layer, group):
        heads = [pl.ds((group * GROUP + within) * HEAD_DIM, HEAD_DIM) for within in range(GROUP)]
        totals = [mix(layer, columns) for columns in heads]
        for columns, total in zip(heads, totals):
            h[:, columns] = total
        if layer + 1 < LAYERS:
            summed = squares[...]
            for total in totals:
                x = total.astype(jnp.float32)
                summed = summed + x * x
            squares[...] = summed

    def settle(layer, group):
        arrive(layer, group, REACH - 1)
        for piece in pieces_of(group):
            slots[layer * PIECES + piece].wait()
        kcat[pl.ds(0, RESP), :] = chosen(layer, 2 * group)
        kcat[pl.ds(RESP, RESP), :] = own[layer, :, pl.ds(group * HEAD_DIM, HEAD_DIM)]
        vcat[pl.ds(0, RESP), pl.ds(0, HEAD_DIM)] = chosen(layer, 2 * group + 1)
        vcat[pl.ds(RESP, RESP), pl.ds(0, HEAD_DIM)] = own[layer, :, pl.ds(HALF + group * HEAD_DIM, HEAD_DIM)]

    def prepare():
        for copy in slots:
            copy.start()
        vcat[:, pl.ds(HEAD_DIM, HEAD_DIM)] = jnp.ones((2 * RESP, HEAD_DIM), jnp.bfloat16)
        for copy in loads:
            copy.wait()
        row = lax.broadcasted_iota(jnp.int32, (RESP, RESP), 0)
        key = lax.broadcasted_iota(jnp.int32, (RESP, RESP), 1)
        seen = (key <= row) & (key < length[0])
        bias[:, pl.ds(0, RESP)] = jnp.zeros((RESP, RESP), jnp.float32)
        bias[:, pl.ds(RESP, RESP)] = jnp.where(seen, 0.0, -1e30)
        add_squares()
        settle_norm()
        squares[...] = jnp.zeros_like(squares)

    def first(group):
        settle(0, group)
        attend(0, group)
        if group == KV_HEADS - 1:
            settle_norm()

    def second(group):
        settle(1, group)
        attend(1, group)
        handed(group).start()

    @pl.when(jnp.logical_not(odd) & (dp < owners - 1))
    def _():
        pl.semaphore_wait(turn, 1)

    for index, (layer, group, step) in enumerate(SLOTS):
        forward(layer, group, step)
        if index == 7:
            @pl.when(odd & (dp < owners - 1))
            def _():
                for slot in SLOTS[:HEAD_START]:
                    for piece in pieces_of(slot[1]):
                        hop(slot[0], piece, 1).wait_send()
                pl.semaphore_signal(turn, inc=1, device_id=back, device_id_type=MESH)
        if index == 7:
            prepare()
        if index >= LAG:
            relay(*SLOTS[index - LAG])
    for slot in SLOTS[len(SLOTS) - LAG :]:
        relay(*slot)
    for group in range(KV_HEADS):
        first(group)
    for group in range(KV_HEADS):
        second(group)

    for slot in SLOTS:
        sent(*slot)
        relay(*slot, sent=True)
    for part in range(OUT_PARTS):
        handed(part).wait()


def per_device(hidden_in, norm_gain, self_kv, prefix_kv, partner_prefix, resp_len):
    hbm = pl.BlockSpec(memory_space=pltpu.HBM)
    bf16, f32 = jnp.bfloat16, jnp.float32
    smem = pl.BlockSpec(memory_space=pltpu.SMEM)
    large = [
        pltpu.with_memory_space_constraint(array, pltpu.HBM)
        for array in (hidden_in, norm_gain, self_kv, prefix_kv)
    ]
    return pl.pallas_call(
        kernel,
        out_shape=pltpu.VMEM((1, RESP, WIN), bf16),
        in_specs=[hbm] * 4 + [smem] * 2,
        out_specs=pl.BlockSpec(memory_space=pltpu.VMEM),
        scratch_shapes=[
            pltpu.VMEM((RESP, WIN), bf16),
            pltpu.VMEM((LAYERS, RESP, KVW), bf16),
            pltpu.VMEM((LAYERS, WIN), f32),
            pltpu.VMEM((LAYERS, PIECES, REACH, RESP, HEAD_DIM), bf16),
            pltpu.VMEM((2 * RESP, HEAD_DIM), bf16),
            pltpu.VMEM((2 * RESP, 2 * HEAD_DIM), bf16),
            pltpu.VMEM((RESP, 2 * RESP), f32),
            pltpu.VMEM((RESP, HEAD_DIM), f32),
            pltpu.VMEM((RESP, HEAD_DIM), f32),
            pltpu.VMEM((LAYERS, PIECES, REACH - 1, RESP, HEAD_DIM), bf16),
            pltpu.SemaphoreType.REGULAR,
            pltpu.SemaphoreType.DMA((3,)),
            pltpu.SemaphoreType.DMA((LAYERS, PIECES)),
            pltpu.SemaphoreType.DMA((LAYERS, PIECES, REACH - 1)),
            pltpu.SemaphoreType.DMA((LAYERS, PIECES, REACH - 1)),
            pltpu.SemaphoreType.DMA((LAYERS, PIECES, REACH - 1)),
            pltpu.SemaphoreType.DMA((LAYERS, PIECES, REACH - 1)),
            pltpu.SemaphoreType.DMA((OUT_PARTS,)),
            pltpu.SemaphoreType.DMA((OUT_PARTS,)),
        ],
        compiler_params=pltpu.CompilerParams(
            collective_id=0, has_side_effects=True, vmem_limit_bytes=48 * 2**20
        ),
        name="judge",
    )(*large, partner_prefix, resp_len)


def solution(mesh):
    return jax.shard_map(
        per_device,
        mesh=mesh,
        in_specs=(
            P("pipe", "dp", None),
            P("pipe", None, None),
            P("pipe", None, "dp", None),
            P("pipe", None, "dp", None),
            P("dp"),
            P("dp"),
        ),
        out_specs=P("pipe", "dp", None),
        check_vma=False,
    )
```

```python
import math

import jax
import jax.numpy as jnp
from jax import lax
from jax.experimental import pallas as pl
from jax.experimental.pallas import tpu as pltpu
from jax.sharding import PartitionSpec as P

HEADS = 32
KV_HEADS = 4
GROUP = HEADS // KV_HEADS
HEAD_DIM = 128
LAYERS = 2
REACH = 4
RESP = 128
WIN = HEADS * HEAD_DIM
KVW = 2 * KV_HEADS * HEAD_DIM
HALF = KVW // 2
PIECES = 2 * KV_HEADS
SCALE = math.log2(math.e) / math.sqrt(HEAD_DIM)
OUT_PARTS = KV_HEADS
PART = WIN // OUT_PARTS
MESH = pl.DeviceIdType.MESH
DEPTH = 16
WAYS = 4
LAG = 2
HEAD_START = 5
SLOTS = [(layer, group, step) for step in range(1, REACH) for layer in range(LAYERS) for group in range(KV_HEADS)]


def kernel(hid_ref, gain_ref, own_ref, pre_ref, partner, length, out_ref,
           h, own, gain, pre, kcat, vcat, bias, squares, factor,
           way, turn, ready, load_sem, slot_sem, send_sem, recv_sem, way_send, way_recv, out_send, out_recv):
    pipe, dp = lax.axis_index("pipe"), lax.axis_index("dp")
    sections, owners = lax.axis_size("pipe"), lax.axis_size("dp")
    right = (pipe, lax.rem(dp + 1, owners))
    left = (pipe, lax.rem(dp + owners - 1, owners))
    below = (pipe, lax.rem(dp + DEPTH, owners))
    above = (pipe, lax.rem(dp + owners - DEPTH, owners))
    start_of_row = (pipe, lax.rem(dp + owners - DEPTH + 1, owners))
    onward = (lax.rem(pipe + 1, sections), dp)
    back = (lax.rem(pipe + sections - 1, sections), dp)

    y, z = dp // DEPTH, dp % DEPTH
    low, high = z == 0, z == DEPTH - 1
    flows = high & (dp < owners - 1)
    relays = high & (y > 0)

    barrier = pltpu.get_barrier_semaphore()
    odd = pipe % 2 == 1
    even = jnp.logical_not(odd)
    pl.semaphore_signal(barrier, inc=1, device_id=onward, device_id_type=MESH)

    @pl.when(odd)
    def _():
        pl.semaphore_signal(barrier, inc=1, device_id=back, device_id_type=MESH)

    @pl.when(dp > 0)
    def _():
        pl.semaphore_signal(barrier, inc=1, device_id=left, device_id_type=MESH)

    @pl.when(relays)
    def _():
        pl.semaphore_signal(barrier, inc=1, device_id=above, device_id_type=MESH)

    @pl.when(low & (y > 0))
    def _():
        pl.semaphore_signal(barrier, inc=1, device_id=(pipe, dp + DEPTH - 1), device_id_type=MESH)

    def column(piece):
        return (piece % 2) * HALF + (piece // 2) * HEAD_DIM

    def owned(layer, piece):
        return pre_ref.at[0, layer, :, pl.ds(column(piece), HEAD_DIM)]

    loads = [
        pltpu.make_async_copy(hid_ref.at[0], h, load_sem.at[0]),
        pltpu.make_async_copy(gain_ref.at[0], gain, load_sem.at[1]),
        pltpu.make_async_copy(own_ref.at[0], own, load_sem.at[2]),
    ]
    slots = [
        pltpu.make_async_copy(owned(layer, piece), pre.at[layer, piece, 0], slot_sem.at[layer, piece])
        for layer in range(LAYERS)
        for piece in range(PIECES)
    ]
    for copy in loads:
        copy.start()
    greeted = 1 + sum(condition.astype(jnp.int32) for condition in (even, dp < owners - 1, flows, relays))
    pl.semaphore_wait(barrier, greeted)

    @pl.when(even)
    def _():
        pl.semaphore_signal(ready, inc=1, device_id=back, device_id_type=MESH)

    def hop(layer, piece, step):
        source = owned(layer, piece) if step == 1 else pre.at[layer, piece, step - 1]
        return pltpu.make_async_remote_copy(
            src_ref=source,
            dst_ref=pre.at[layer, piece, step],
            send_sem=send_sem.at[layer, piece, step - 1],
            recv_sem=recv_sem.at[layer, piece, step - 1],
            device_id=right,
            device_id_type=MESH,
        )

    def aside(layer, piece, step):
        source = owned(layer, piece) if step == 1 else pre.at[layer, piece, step - 1]
        return pltpu.make_async_remote_copy(
            src_ref=source,
            dst_ref=way.at[layer, piece, step - 1],
            send_sem=send_sem.at[layer, piece, step - 1],
            recv_sem=way_recv.at[layer, piece, step - 1],
            device_id=below,
            device_id_type=MESH,
        )

    def relayed(layer, piece, step):
        return pltpu.make_async_remote_copy(
            src_ref=way.at[layer, piece, step - 1],
            dst_ref=pre.at[layer, piece, step],
            send_sem=way_send.at[layer, piece, step - 1],
            recv_sem=recv_sem.at[layer, piece, step - 1],
            device_id=start_of_row,
            device_id_type=MESH,
        )

    def pieces_of(group):
        return 2 * group, 2 * group + 1

    def arrive(layer, group, step):
        @pl.when(dp >= step)
        def _():
            for piece in pieces_of(group):
                hop(layer, piece, step).wait_recv()

    def forward(layer, group, step):
        if step > 1:
            arrive(layer, group, step - 1)

        @pl.when((dp >= step - 1) & (z < DEPTH - 1))
        def _():
            for piece in pieces_of(group):
                hop(layer, piece, step).start()

        @pl.when(flows)
        def _():
            for piece in pieces_of(group):
                rank = piece % WAYS

                @pl.when(y < rank)
                def _():
                    hop(layer, piece, step).start()

                if rank < WAYS - 1:

                    @pl.when(y >= rank)
                    def _():
                        aside(layer, piece, step).start()

    def relay(layer, group, step, sent=False):
        @pl.when(relays)
        def _():
            for piece in pieces_of(group):
                rank = piece % WAYS
                if rank < WAYS - 1:

                    @pl.when(y > rank)
                    def _():
                        if sent:
                            relayed(layer, piece, step).wait_send()
                        else:
                            aside(layer, piece, step).wait_recv()
                            relayed(layer, piece, step).start()

    def sent(layer, group, step):
        early = step == 1 and (layer, group, step) in SLOTS[:HEAD_START]
        @pl.when((dp >= step - 1) & (dp < owners - 1) & (jnp.logical_not(odd) if early else True))
        def _():
            for piece in pieces_of(group):
                hop(layer, piece, step).wait_send()

    def handed(part):
        columns = pl.ds(part * PART, PART)
        return pltpu.make_async_remote_copy(
            src_ref=h.at[:, columns],
            dst_ref=out_ref.at[0, :, columns],
            send_sem=out_send.at[part],
            recv_sem=out_recv.at[part],
            device_id=onward,
            device_id_type=MESH,
        )

    def head_columns(head):
        return pl.ds(pl.multiple_of(head * HEAD_DIM, HEAD_DIM), HEAD_DIM)

    def add_squares():
        squares[...] = jnp.zeros_like(squares)

        @pl.loop(0, HEADS // GROUP)
        def _(group):
            summed = squares[...]
            for within in range(GROUP):
                x = h[:, head_columns(group * GROUP + within)].astype(jnp.float32)
                summed = summed + x * x
            squares[...] = summed

    def settle_norm():
        mean = jnp.sum(squares[...], axis=-1, keepdims=True) * (1.0 / WIN)
        factor[...] = jnp.broadcast_to(lax.rsqrt(mean + 1e-05), (RESP, HEAD_DIM))

    def chosen(layer, piece):
        offset = dp - partner[0]
        block = pre[layer, piece, 0]
        for step in range(1, REACH):
            block = jnp.where(offset == step, pre[layer, piece, step], block)
        return block

    def mix(layer, columns):
        x = h[:, columns].astype(jnp.float32)
        query = (x * factor[...] * gain[pl.ds(layer, 1), columns]).astype(jnp.bfloat16)
        scores = lax.dot_general(
            query, kcat[...], (((1,), (1,)), ((), ())), preferred_element_type=jnp.float32
        )
        scores = scores * SCALE + bias[...]
        top = jnp.max(scores, axis=-1, keepdims=True)
        expo = jnp.exp2(scores - top).astype(jnp.bfloat16)
        mixed = jnp.dot(expo, vcat[...], preferred_element_type=jnp.float32)
        return (x + mixed[:, :HEAD_DIM] / mixed[:, HEAD_DIM:]).astype(jnp.bfloat16)

    def attend(layer, group):
        heads = [pl.ds((group * GROUP + within) * HEAD_DIM, HEAD_DIM) for within in range(GROUP)]
        totals = [mix(layer, columns) for columns in heads]
        for columns, total in zip(heads, totals):
            h[:, columns] = total
        if layer + 1 < LAYERS:
            summed = squares[...]
            for total in totals:
                x = total.astype(jnp.float32)
                summed = summed + x * x
            squares[...] = summed

    def settle(layer, group):
        arrive(layer, group, REACH - 1)
        for piece in pieces_of(group):
            slots[layer * PIECES + piece].wait()
        kcat[pl.ds(0, RESP), :] = chosen(layer, 2 * group)
        kcat[pl.ds(RESP, RESP), :] = own[layer, :, pl.ds(group * HEAD_DIM, HEAD_DIM)]
        vcat[pl.ds(0, RESP), pl.ds(0, HEAD_DIM)] = chosen(layer, 2 * group + 1)
        vcat[pl.ds(RESP, RESP), pl.ds(0, HEAD_DIM)] = own[layer, :, pl.ds(HALF + group * HEAD_DIM, HEAD_DIM)]

    def prepare():
        for copy in slots:
            copy.start()
        vcat[:, pl.ds(HEAD_DIM, HEAD_DIM)] = jnp.ones((2 * RESP, HEAD_DIM), jnp.bfloat16)
        for copy in loads:
            copy.wait()
        row = lax.broadcasted_iota(jnp.int32, (RESP, RESP), 0)
        key = lax.broadcasted_iota(jnp.int32, (RESP, RESP), 1)
        seen = (key <= row) & (key < length[0])
        bias[:, pl.ds(0, RESP)] = jnp.zeros((RESP, RESP), jnp.float32)
        bias[:, pl.ds(RESP, RESP)] = jnp.where(seen, 0.0, -1e30)
        add_squares()
        settle_norm()
        squares[...] = jnp.zeros_like(squares)

    def first(group):
        settle(0, group)
        attend(0, group)
        if group == KV_HEADS - 1:
            settle_norm()

    def second(group):
        settle(1, group)
        attend(1, group)
        handed(group).start()

    @pl.when(even & (dp < owners - 1))
    def _():
        pl.semaphore_wait(turn, 1)

    for index, (layer, group, step) in enumerate(SLOTS):
        forward(layer, group, step)
        if index == 7:
            @pl.when(odd & (dp < owners - 1))
            def _():
                for slot in SLOTS[:HEAD_START]:
                    for piece in pieces_of(slot[1]):
                        hop(slot[0], piece, 1).wait_send()
                pl.semaphore_signal(turn, inc=1, device_id=back, device_id_type=MESH)
        if index == 7:
            prepare()
        if index >= LAG:
            relay(*SLOTS[index - LAG])
    for slot in SLOTS[len(SLOTS) - LAG :]:
        relay(*slot)
    for group in range(KV_HEADS):
        first(group)

    @pl.when(odd)
    def _():
        pl.semaphore_wait(ready, 1)

    for group in range(KV_HEADS):
        second(group)

    for slot in SLOTS:
        sent(*slot)
        relay(*slot, sent=True)
    for part in range(OUT_PARTS):
        handed(part).wait()


def per_device(hidden_in, norm_gain, self_kv, prefix_kv, partner_prefix, resp_len):
    hbm = pl.BlockSpec(memory_space=pltpu.HBM)
    bf16, f32 = jnp.bfloat16, jnp.float32
    smem = pl.BlockSpec(memory_space=pltpu.SMEM)
    large = [
        pltpu.with_memory_space_constraint(array, pltpu.HBM)
        for array in (hidden_in, norm_gain, self_kv, prefix_kv)
    ]
    return pl.pallas_call(
        kernel,
        out_shape=pltpu.VMEM((1, RESP, WIN), bf16),
        in_specs=[hbm] * 4 + [smem] * 2,
        out_specs=pl.BlockSpec(memory_space=pltpu.VMEM),
        scratch_shapes=[
            pltpu.VMEM((RESP, WIN), bf16),
            pltpu.VMEM((LAYERS, RESP, KVW), bf16),
            pltpu.VMEM((LAYERS, WIN), f32),
            pltpu.VMEM((LAYERS, PIECES, REACH, RESP, HEAD_DIM), bf16),
            pltpu.VMEM((2 * RESP, HEAD_DIM), bf16),
            pltpu.VMEM((2 * RESP, 2 * HEAD_DIM), bf16),
            pltpu.VMEM((RESP, 2 * RESP), f32),
            pltpu.VMEM((RESP, HEAD_DIM), f32),
            pltpu.VMEM((RESP, HEAD_DIM), f32),
            pltpu.VMEM((LAYERS, PIECES, REACH - 1, RESP, HEAD_DIM), bf16),
            pltpu.SemaphoreType.REGULAR,
            pltpu.SemaphoreType.REGULAR,
            pltpu.SemaphoreType.DMA((3,)),
            pltpu.SemaphoreType.DMA((LAYERS, PIECES)),
            pltpu.SemaphoreType.DMA((LAYERS, PIECES, REACH - 1)),
            pltpu.SemaphoreType.DMA((LAYERS, PIECES, REACH - 1)),
            pltpu.SemaphoreType.DMA((LAYERS, PIECES, REACH - 1)),
            pltpu.SemaphoreType.DMA((LAYERS, PIECES, REACH - 1)),
            pltpu.SemaphoreType.DMA((OUT_PARTS,)),
            pltpu.SemaphoreType.DMA((OUT_PARTS,)),
        ],
        compiler_params=pltpu.CompilerParams(
            collective_id=0, has_side_effects=True, vmem_limit_bytes=48 * 2**20
        ),
        name="judge",
    )(*large, partner_prefix, resp_len)


def solution(mesh):
    return jax.shard_map(
        per_device,
        mesh=mesh,
        in_specs=(
            P("pipe", "dp", None),
            P("pipe", None, None),
            P("pipe", None, "dp", None),
            P("pipe", None, "dp", None),
            P("dp"),
            P("dp"),
        ),
        out_specs=P("pipe", "dp", None),
        check_vma=False,
    )
```

```python
import math

import jax
import jax.numpy as jnp
from jax import lax
from jax.experimental import pallas as pl
from jax.experimental.pallas import tpu as pltpu
from jax.sharding import PartitionSpec as P

HEADS = 32
KV_HEADS = 4
GROUP = HEADS // KV_HEADS
HEAD_DIM = 128
LAYERS = 2
REACH = 4
RESP = 128
WIN = HEADS * HEAD_DIM
KVW = 2 * KV_HEADS * HEAD_DIM
HALF = KVW // 2
PIECES = 2 * KV_HEADS
SCALE = math.log2(math.e) / math.sqrt(HEAD_DIM)
OUT_PARTS = 2 * KV_HEADS
PART = WIN // OUT_PARTS
MESH = pl.DeviceIdType.MESH
DEPTH = 16
WAYS = 4
LAG = 2
HEAD_START = 5
SLOTS = [(layer, group, step) for step in range(1, REACH) for layer in range(LAYERS) for group in range(KV_HEADS)]


def kernel(hid_ref, gain_ref, own_ref, pre_ref, partner, length, out_ref,
           h, own, gain, pre, kcat, vcat, bias, squares, factor,
           way, turn, ready, load_sem, slot_sem, send_sem, recv_sem, way_send, way_recv, out_send, out_recv):
    pipe, dp = lax.axis_index("pipe"), lax.axis_index("dp")
    sections, owners = lax.axis_size("pipe"), lax.axis_size("dp")
    right = (pipe, lax.rem(dp + 1, owners))
    left = (pipe, lax.rem(dp + owners - 1, owners))
    below = (pipe, lax.rem(dp + DEPTH, owners))
    above = (pipe, lax.rem(dp + owners - DEPTH, owners))
    start_of_row = (pipe, lax.rem(dp + owners - DEPTH + 1, owners))
    onward = (lax.rem(pipe + 1, sections), dp)
    back = (lax.rem(pipe + sections - 1, sections), dp)

    y, z = dp // DEPTH, dp % DEPTH
    low, high = z == 0, z == DEPTH - 1
    flows = high & (dp < owners - 1)
    relays = high & (y > 0)

    barrier = pltpu.get_barrier_semaphore()
    odd = pipe % 2 == 1
    even = jnp.logical_not(odd)
    pl.semaphore_signal(barrier, inc=1, device_id=onward, device_id_type=MESH)

    @pl.when(odd)
    def _():
        pl.semaphore_signal(barrier, inc=1, device_id=back, device_id_type=MESH)

    @pl.when(dp > 0)
    def _():
        pl.semaphore_signal(barrier, inc=1, device_id=left, device_id_type=MESH)

    @pl.when(relays)
    def _():
        pl.semaphore_signal(barrier, inc=1, device_id=above, device_id_type=MESH)

    @pl.when(low & (y > 0))
    def _():
        pl.semaphore_signal(barrier, inc=1, device_id=(pipe, dp + DEPTH - 1), device_id_type=MESH)

    def column(piece):
        return (piece % 2) * HALF + (piece // 2) * HEAD_DIM

    def owned(layer, piece):
        return pre_ref.at[0, layer, :, pl.ds(column(piece), HEAD_DIM)]

    loads = [
        pltpu.make_async_copy(hid_ref.at[0], h, load_sem.at[0]),
        pltpu.make_async_copy(gain_ref.at[0], gain, load_sem.at[1]),
        pltpu.make_async_copy(own_ref.at[0], own, load_sem.at[2]),
    ]
    slots = [
        pltpu.make_async_copy(owned(layer, piece), pre.at[layer, piece, 0], slot_sem.at[layer, piece])
        for layer in range(LAYERS)
        for piece in range(PIECES)
    ]
    for copy in loads:
        copy.start()
    greeted = 1 + sum(condition.astype(jnp.int32) for condition in (even, dp < owners - 1, flows, relays))
    pl.semaphore_wait(barrier, greeted)

    @pl.when(even)
    def _():
        pl.semaphore_signal(ready, inc=1, device_id=back, device_id_type=MESH)

    def hop(layer, piece, step):
        source = owned(layer, piece) if step == 1 else pre.at[layer, piece, step - 1]
        return pltpu.make_async_remote_copy(
            src_ref=source,
            dst_ref=pre.at[layer, piece, step],
            send_sem=send_sem.at[layer, piece, step - 1],
            recv_sem=recv_sem.at[layer, piece, step - 1],
            device_id=right,
            device_id_type=MESH,
        )

    def aside(layer, piece, step):
        source = owned(layer, piece) if step == 1 else pre.at[layer, piece, step - 1]
        return pltpu.make_async_remote_copy(
            src_ref=source,
            dst_ref=way.at[layer, piece, step - 1],
            send_sem=send_sem.at[layer, piece, step - 1],
            recv_sem=way_recv.at[layer, piece, step - 1],
            device_id=below,
            device_id_type=MESH,
        )

    def relayed(layer, piece, step):
        return pltpu.make_async_remote_copy(
            src_ref=way.at[layer, piece, step - 1],
            dst_ref=pre.at[layer, piece, step],
            send_sem=way_send.at[layer, piece, step - 1],
            recv_sem=recv_sem.at[layer, piece, step - 1],
            device_id=start_of_row,
            device_id_type=MESH,
        )

    def pieces_of(group):
        return 2 * group, 2 * group + 1

    def arrive(layer, group, step):
        @pl.when(dp >= step)
        def _():
            for piece in pieces_of(group):
                hop(layer, piece, step).wait_recv()

    def forward(layer, group, step):
        if step > 1:
            arrive(layer, group, step - 1)

        @pl.when((dp >= step - 1) & (z < DEPTH - 1))
        def _():
            for piece in pieces_of(group):
                hop(layer, piece, step).start()

        @pl.when(flows)
        def _():
            for piece in pieces_of(group):
                rank = piece % WAYS

                @pl.when(y < rank)
                def _():
                    hop(layer, piece, step).start()

                if rank < WAYS - 1:

                    @pl.when(y >= rank)
                    def _():
                        aside(layer, piece, step).start()

    def relay(layer, group, step, sent=False):
        @pl.when(relays)
        def _():
            for piece in pieces_of(group):
                rank = piece % WAYS
                if rank < WAYS - 1:

                    @pl.when(y > rank)
                    def _():
                        if sent:
                            relayed(layer, piece, step).wait_send()
                        else:
                            aside(layer, piece, step).wait_recv()
                            relayed(layer, piece, step).start()

    def sent(layer, group, step):
        early = step == 1 and (layer, group, step) in SLOTS[:HEAD_START]
        @pl.when((dp >= step - 1) & (dp < owners - 1) & (jnp.logical_not(odd) if early else True))
        def _():
            for piece in pieces_of(group):
                hop(layer, piece, step).wait_send()

    def handed(part):
        columns = pl.ds(part * PART, PART)
        return pltpu.make_async_remote_copy(
            src_ref=h.at[:, columns],
            dst_ref=out_ref.at[0, :, columns],
            send_sem=out_send.at[part],
            recv_sem=out_recv.at[part],
            device_id=onward,
            device_id_type=MESH,
        )

    def head_columns(head):
        return pl.ds(pl.multiple_of(head * HEAD_DIM, HEAD_DIM), HEAD_DIM)

    def add_squares():
        squares[...] = jnp.zeros_like(squares)

        @pl.loop(0, HEADS // GROUP)
        def _(group):
            summed = squares[...]
            for within in range(GROUP):
                x = h[:, head_columns(group * GROUP + within)].astype(jnp.float32)
                summed = summed + x * x
            squares[...] = summed

    def settle_norm():
        mean = jnp.sum(squares[...], axis=-1, keepdims=True) * (1.0 / WIN)
        factor[...] = jnp.broadcast_to(lax.rsqrt(mean + 1e-05), (RESP, HEAD_DIM))

    def chosen(layer, piece):
        offset = dp - partner[0]
        block = pre[layer, piece, 0]
        for step in range(1, REACH):
            block = jnp.where(offset == step, pre[layer, piece, step], block)
        return block

    def mix(layer, columns):
        x = h[:, columns].astype(jnp.float32)
        query = (x * factor[...] * gain[pl.ds(layer, 1), columns]).astype(jnp.bfloat16)
        scores = lax.dot_general(
            query, kcat[...], (((1,), (1,)), ((), ())), preferred_element_type=jnp.float32
        )
        scores = scores * SCALE + bias[...]
        top = jnp.max(scores, axis=-1, keepdims=True)
        expo = jnp.exp2(scores - top).astype(jnp.bfloat16)
        mixed = jnp.dot(expo, vcat[...], preferred_element_type=jnp.float32)
        return (x + mixed[:, :HEAD_DIM] / mixed[:, HEAD_DIM:]).astype(jnp.bfloat16)

    def attend(layer, group, first=0, last=GROUP):
        heads = [pl.ds((group * GROUP + within) * HEAD_DIM, HEAD_DIM) for within in range(first, last)]
        totals = [mix(layer, columns) for columns in heads]
        for columns, total in zip(heads, totals):
            h[:, columns] = total
        if layer + 1 < LAYERS:
            summed = squares[...]
            for total in totals:
                x = total.astype(jnp.float32)
                summed = summed + x * x
            squares[...] = summed

    def settle(layer, group):
        arrive(layer, group, REACH - 1)
        for piece in pieces_of(group):
            slots[layer * PIECES + piece].wait()
        kcat[pl.ds(0, RESP), :] = chosen(layer, 2 * group)
        kcat[pl.ds(RESP, RESP), :] = own[layer, :, pl.ds(group * HEAD_DIM, HEAD_DIM)]
        vcat[pl.ds(0, RESP), pl.ds(0, HEAD_DIM)] = chosen(layer, 2 * group + 1)
        vcat[pl.ds(RESP, RESP), pl.ds(0, HEAD_DIM)] = own[layer, :, pl.ds(HALF + group * HEAD_DIM, HEAD_DIM)]

    def prepare():
        for copy in slots:
            copy.start()
        vcat[:, pl.ds(HEAD_DIM, HEAD_DIM)] = jnp.ones((2 * RESP, HEAD_DIM), jnp.bfloat16)
        for copy in loads:
            copy.wait()
        row = lax.broadcasted_iota(jnp.int32, (RESP, RESP), 0)
        key = lax.broadcasted_iota(jnp.int32, (RESP, RESP), 1)
        seen = (key <= row) & (key < length[0])
        bias[:, pl.ds(0, RESP)] = jnp.zeros((RESP, RESP), jnp.float32)
        bias[:, pl.ds(RESP, RESP)] = jnp.where(seen, 0.0, -1e30)
        add_squares()
        settle_norm()
        squares[...] = jnp.zeros_like(squares)

    def first(group):
        settle(0, group)
        attend(0, group)
        if group == KV_HEADS - 1:
            settle_norm()

    def second(group):
        settle(1, group)
        pace = GROUP // 2 if group == KV_HEADS - 1 else GROUP
        for begin in range(0, GROUP, pace):
            attend(1, group, begin, begin + pace)
            for head in range(begin, begin + pace, GROUP // 2):
                handed((group * GROUP + head) * OUT_PARTS // HEADS).start()

    @pl.when(even & (dp < owners - 1))
    def _():
        pl.semaphore_wait(turn, 1)

    for index, (layer, group, step) in enumerate(SLOTS):
        forward(layer, group, step)
        if index == 7:
            @pl.when(odd & (dp < owners - 1))
            def _():
                for slot in SLOTS[:HEAD_START]:
                    for piece in pieces_of(slot[1]):
                        hop(slot[0], piece, 1).wait_send()
                pl.semaphore_signal(turn, inc=1, device_id=back, device_id_type=MESH)
        if index == 7:
            prepare()
        if index >= LAG:
            relay(*SLOTS[index - LAG])
    for slot in SLOTS[len(SLOTS) - LAG :]:
        relay(*slot)
    for group in range(KV_HEADS):
        first(group)

    @pl.when(odd)
    def _():
        pl.semaphore_wait(ready, 1)

    for group in range(KV_HEADS):
        second(group)

    for slot in SLOTS:
        sent(*slot)
        relay(*slot, sent=True)
    for part in range(OUT_PARTS):
        handed(part).wait()


def per_device(hidden_in, norm_gain, self_kv, prefix_kv, partner_prefix, resp_len):
    hbm = pl.BlockSpec(memory_space=pltpu.HBM)
    bf16, f32 = jnp.bfloat16, jnp.float32
    smem = pl.BlockSpec(memory_space=pltpu.SMEM)
    large = [
        pltpu.with_memory_space_constraint(array, pltpu.HBM)
        for array in (hidden_in, norm_gain, self_kv, prefix_kv)
    ]
    return pl.pallas_call(
        kernel,
        out_shape=pltpu.VMEM((1, RESP, WIN), bf16),
        in_specs=[hbm] * 4 + [smem] * 2,
        out_specs=pl.BlockSpec(memory_space=pltpu.VMEM),
        scratch_shapes=[
            pltpu.VMEM((RESP, WIN), bf16),
            pltpu.VMEM((LAYERS, RESP, KVW), bf16),
            pltpu.VMEM((LAYERS, WIN), f32),
            pltpu.VMEM((LAYERS, PIECES, REACH, RESP, HEAD_DIM), bf16),
            pltpu.VMEM((2 * RESP, HEAD_DIM), bf16),
            pltpu.VMEM((2 * RESP, 2 * HEAD_DIM), bf16),
            pltpu.VMEM((RESP, 2 * RESP), f32),
            pltpu.VMEM((RESP, HEAD_DIM), f32),
            pltpu.VMEM((RESP, HEAD_DIM), f32),
            pltpu.VMEM((LAYERS, PIECES, REACH - 1, RESP, HEAD_DIM), bf16),
            pltpu.SemaphoreType.REGULAR,
            pltpu.SemaphoreType.REGULAR,
            pltpu.SemaphoreType.DMA((3,)),
            pltpu.SemaphoreType.DMA((LAYERS, PIECES)),
            pltpu.SemaphoreType.DMA((LAYERS, PIECES, REACH - 1)),
            pltpu.SemaphoreType.DMA((LAYERS, PIECES, REACH - 1)),
            pltpu.SemaphoreType.DMA((LAYERS, PIECES, REACH - 1)),
            pltpu.SemaphoreType.DMA((LAYERS, PIECES, REACH - 1)),
            pltpu.SemaphoreType.DMA((OUT_PARTS,)),
            pltpu.SemaphoreType.DMA((OUT_PARTS,)),
        ],
        compiler_params=pltpu.CompilerParams(
            collective_id=0, has_side_effects=True, vmem_limit_bytes=48 * 2**20
        ),
        name="judge",
    )(*large, partner_prefix, resp_len)


def solution(mesh):
    return jax.shard_map(
        per_device,
        mesh=mesh,
        in_specs=(
            P("pipe", "dp", None),
            P("pipe", None, None),
            P("pipe", None, "dp", None),
            P("pipe", None, "dp", None),
            P("dp"),
            P("dp"),
        ),
        out_specs=P("pipe", "dp", None),
        check_vma=False,
    )
```
